512 devices in a mesh: section: 32 (over x_hi, z), tensor: 4 (over y), dp: 4 (over x_lo, core).
Axes of the slice: x: 4 (x_hi: 2, x_lo: 2; x = x_hi * 2 + x_lo), y: 4, z: 16, core: 2. Of those that a mesh axis runs over, the one named last changes fastest.
Arguments:
- sent_acts: bfloat16 [32, 256, 3072], P('section', ('tensor', 'dp')), may hold values from -36 to 36
- sent_grads: bfloat16 [32, 256, 3072], P('section', ('tensor', 'dp')), may hold values from -0.375 to 0.375
- saved_inputs: bfloat16 [32, 256, 3072], P('section', ('tensor', 'dp')), may hold values from -36 to 36
- w_in: bfloat16 [32, 3072, 3072], P('section', None, ('tensor', 'dp')), may hold values from -0.109375 to 0.109375
- w_out: bfloat16 [32, 3072, 3072], P('section', ('tensor', 'dp')), may hold values from -0.078125 to 0.078125
Outputs:
- out_acts: bfloat16 [32, 256, 3072], P('section', ('tensor', 'dp'))
- out_grads: bfloat16 [32, 256, 3072], P('section', ('tensor', 'dp'))
- grad_in: bfloat16 [32, 3072, 3072], P('section', None, ('tensor', 'dp'))
- grad_out: bfloat16 [32, 3072, 3072], P('section', ('tensor', 'dp'))
The draws below stay inside these ranges and needn't reach their ends.
All inputs are finite; a program needn't handle non-finite values.
Results may differ from the reference program's by a relative error of at most 0.015.
Values may be sent and summed in bfloat16 or wider, within the bound.
A program may use at most 64 MiB of HBM per device.

```python
import math
import jax
import jax.numpy as jnp
from jax import lax

D = 3072
HID = 1536
FFW = 6144
SLOTW = 3072
TOKENS = 256
N_SECTION = 32
N_TENSOR = 4
N_DP = 4


def scaled_field(key, low_scale, high_scale, clip_level):
    base_key, row_key, col_key = jax.random.split(key, 3)
    row_scale = jnp.exp(jax.random.uniform(row_key, (N_SECTION, TOKENS, 1), jnp.float32, math.log(low_scale), math.log(high_scale)))
    col_scale = jnp.exp(jax.random.uniform(col_key, (N_SECTION, 1, D), jnp.float32, math.log(0.3), math.log(3.0)))
    base_values = jax.random.normal(base_key, (N_SECTION, TOKENS, D), jnp.float32)
    base_values = jnp.clip(base_values, -clip_level, clip_level)
    return (base_values * row_scale * col_scale).astype(jnp.bfloat16)


def draw_sent_acts(key, part):
    key = jax.random.fold_in(key, 11)
    return scaled_field(key, 0.3, 3.0, 4.0)


def draw_saved_inputs(key, part):
    key = jax.random.fold_in(key, 23)
    return scaled_field(key, 0.3, 3.0, 4.0)


def steps_of(stream_key, extent, cuts, least, largest):
    factor_of, own = 1.0, jax.random.fold_in(stream_key, 6)
    for axis_at, blocks in cuts:
        heights = jnp.exp(jax.random.uniform(jax.random.fold_in(own, axis_at), (blocks,), jnp.float32, least / len(cuts), largest / len(cuts)))
        factor_of = factor_of * jnp.repeat(heights, extent[axis_at] // blocks).reshape([-1 if axis == axis_at else 1 for axis in range(len(extent))])
    return factor_of


def scatter_about(key, shape, scale, bound, pieces=(), kind=jnp.bfloat16):
    gain = steps_of(key, shape, pieces, -0.22, 0.18) if pieces else 1.0
    entries = jax.random.normal(key, shape, jnp.float32) * scale * gain
    return jnp.minimum(jnp.maximum(entries, -bound), bound).astype(kind)


def setup_inputs(seed: int = 0) -> dict:
    arg_keys = jax.random.split(jax.random.key(seed), 6)
    return {
        "sent_acts": draw_sent_acts(jax.random.fold_in(arg_keys[5], 71), 0),
        "sent_grads": scatter_about(arg_keys[1], (N_SECTION, TOKENS, D), 0.0625, 0.375, ((0, 32), (1, 16))),
        "saved_inputs": draw_saved_inputs(jax.random.fold_in(arg_keys[5], 71), 0),
        "w_in": scatter_about(arg_keys[3], (N_SECTION, D, SLOTW), D ** -0.5, 0.109375, ((0, 32), (2, 16))),
        "w_out": scatter_about(arg_keys[4], (N_SECTION, SLOTW, D), FFW ** -0.5, 0.078125, ((0, 32), (1, 16))),
    }


eps = 1e-05

def normalize(features):
    inv_scale = lax.rsqrt(lax.optimization_barrier(jnp.mean(features * features, axis=-1, keepdims=True)) + eps)
    return features * inv_scale

def activate(pre_values):
    return jax.nn.gelu(pre_values, approximate=True)

def group_sum(left_rows, right_rows):
    groups = N_TENSOR * N_DP
    row_total = left_rows.shape[0]
    left_f32 = left_rows.reshape(row_total, groups, -1).astype(jnp.float32)
    right_f32 = right_rows.reshape(groups, left_f32.shape[2], -1).astype(jnp.float32)
    partials = jnp.einsum('rgh,ghd->grd', left_f32, right_f32).astype(jnp.bfloat16)
    return lax.optimization_barrier(jnp.sum(partials.astype(jnp.float32), axis=0))

def row_term(left_rows, right_rows):
    return lax.dot_general(left_rows, right_rows, (((0,), (0,)), ((), ())), preferred_element_type=jnp.float32).astype(jnp.bfloat16)

def reference(sent_acts, sent_grads, saved_inputs, w_in, w_out):
    section_half = N_SECTION // 2
    groups = N_TENSOR * N_DP
    piece_units = HID // (2 * N_DP)
    width_all = groups * 2 * piece_units

    def one_slot(section_index, section_pos, layer_in, layer_out):
        source_row = jnp.where(section_pos == 0, section_index, section_index - 1).astype(jnp.int32)
        target_row = jnp.where(section_pos == section_half - 1, section_index, section_index + 1).astype(jnp.int32)
        inputs = sent_acts[source_row].astype(jnp.float32)
        normed = normalize(inputs).astype(jnp.bfloat16)
        hidden = activate(jnp.dot(normed, layer_in, preferred_element_type=jnp.float32)).astype(jnp.bfloat16)
        forward = (inputs + group_sum(hidden, layer_out)).astype(jnp.bfloat16)
        cotangent = sent_grads[target_row]
        kept_rows = saved_inputs[section_index].astype(jnp.float32)
        normed_b, norm_back = jax.vjp(normalize, kept_rows)
        normed_b = normed_b.astype(jnp.bfloat16)
        pre_act = jnp.dot(normed_b, layer_in, preferred_element_type=jnp.float32)
        hidden_b, act_back = jax.vjp(activate, pre_act)
        hidden_b = hidden_b.astype(jnp.bfloat16)
        d_hidden = lax.dot_general(cotangent, layer_out, (((1,), (1,)), ((), ())), preferred_element_type=jnp.float32)
        d_pre = act_back(d_hidden)[0].astype(jnp.bfloat16)
        d_normed = group_sum(d_pre, layer_in.T)
        backward = (cotangent.astype(jnp.float32) + norm_back(d_normed)[0]).astype(jnp.bfloat16)
        return (forward, backward, row_term(normed_b, d_pre), row_term(hidden_b, cotangent))

    def one_pair(section_pos):
        lower_in = lax.dynamic_index_in_dim(w_in, section_pos, 0, False).reshape(D, groups, piece_units)
        upper_in = lax.dynamic_index_in_dim(w_in, section_pos + section_half, 0, False).reshape(D, groups, piece_units)
        layer_in = jnp.stack([lower_in, upper_in], axis=2).reshape(D, width_all)
        lower_out = lax.dynamic_index_in_dim(w_out, section_pos, 0, False).reshape(groups, piece_units, D)
        upper_out = lax.dynamic_index_in_dim(w_out, section_pos + section_half, 0, False).reshape(groups, piece_units, D)
        layer_out = jnp.stack([lower_out, upper_out], axis=1).reshape(width_all, D)
        fwd_low, bwd_low, tin_low, tout_low = one_slot(section_pos, section_pos, layer_in, layer_out)
        fwd_up, bwd_up, tin_up, tout_up = one_slot(section_pos + section_half, section_pos, layer_in, layer_out)
        total_in = (tin_low.astype(jnp.float32) + tin_up.astype(jnp.float32)).reshape(D, groups, 2, piece_units)
        total_out = (tout_low.astype(jnp.float32) + tout_up.astype(jnp.float32)).reshape(groups, 2, piece_units, D)
        gin = jnp.stack([total_in[:, :, 0].reshape(D, groups * piece_units), total_in[:, :, 1].reshape(D, groups * piece_units)], axis=0).astype(jnp.bfloat16)
        gout = jnp.stack([total_out[:, 0].reshape(groups * piece_units, D), total_out[:, 1].reshape(groups * piece_units, D)], axis=0).astype(jnp.bfloat16)
        return (jnp.stack([fwd_low, fwd_up], axis=0), jnp.stack([bwd_low, bwd_up], axis=0), gin, gout)
    fwd_all, bwd_all, gin_all, gout_all = lax.map(one_pair, jnp.arange(section_half, dtype=jnp.int32))

    def arrange(values):
        moved = jnp.swapaxes(values, 0, 1)
        return moved.reshape((N_SECTION,) + values.shape[2:])
    return (arrange(fwd_all), arrange(bwd_all), arrange(gin_all), arrange(gout_all))
```

```python
import functools

import jax
import jax.numpy as jnp
from jax import lax
from jax.experimental import pallas as pl
from jax.experimental.pallas import tpu as pltpu
from jax.sharding import PartitionSpec as P

MESH = pl.DeviceIdType.MESH
F32, BF16 = jnp.float32, jnp.bfloat16
EPS = 1e-05
NB, CT, NF = 0, 1, 2
BWD, FWD = 0, 1
GELU_A, GELU_B = 0.7978845608028654, 0.044715


def inv_rms(values):
    return lax.rsqrt(jnp.mean(values * values, axis=-1, keepdims=True) + EPS)


def gelu(v):
    return 0.5 * v * (1.0 + jnp.tanh(GELU_A * (v + GELU_B * (v * v * v))))


def gelu_and_slope(v):
    square = v * v
    t = jnp.tanh(GELU_A * (v + GELU_B * (v * square)))
    value = 0.5 * v * (1.0 + t)
    slope = 0.5 * (1.0 + t) + 0.5 * v * (1.0 - t * t) * (GELU_A * (1.0 + 3.0 * GELU_B * square))
    return value, slope


def nn(a, b):
    return jnp.dot(a, b, preferred_element_type=F32)


def nt(a, b):
    return lax.dot_general(a, b, (((1,), (1,)), ((), ())), preferred_element_type=F32)


def tn(a, b):
    return lax.dot_general(a, b, (((0,), (0,)), ((), ())), preferred_element_type=F32)


def kernel(
    n_z, acts, grads, saved, w_in, w_out, o_acts, o_grads, o_gin, o_gout,
    tok, ag, win, wout, part, r1, r2, r3, r4, q, hid, dpre, slope, gin_s, gin_r, gout_s, gout_r, gin_o, gout_o,
    loc_sem, ag_send, ag_recv, rs_send, rs_recv, ex_send, ex_recv,
):
    sec, y, dp = lax.axis_index("section"), lax.axis_index("tensor"), lax.axis_index("dp")
    z = lax.rem(sec, n_z)
    x_hi = sec // n_z
    x = 2 * x_hi + dp // 2
    core = lax.rem(dp, 2)
    D = ag.shape[-1]
    H, Q = D // 2, D // 4
    tokens = 16 * ag.shape[3]

    def at(dy, dx):
        return lax.rem(y + dy + 4, 4), lax.rem(x + dx + 4, 4)

    def chip(dy, dx):
        yy, xx = at(dy, dx)
        return ((xx // 2) * n_z + z, yy, 2 * lax.rem(xx, 2) + core)

    def plane(dz):
        return (x_hi * n_z + lax.rem(z + dz + n_z, n_z), y, dp)

    sibling = (sec, y, dp + 1 - 2 * core)

    sent = []

    def send(src, dst, ssem, rsem, dev):
        copy = pltpu.make_async_remote_copy(
            src_ref=src, dst_ref=dst, send_sem=ssem, recv_sem=rsem, device_id=dev, device_id_type=MESH
        )
        copy.start()
        sent.append(copy)
        return copy

    def local(src, dst, i):
        copy = pltpu.make_async_copy(src, dst, loc_sem.at[i])
        copy.start()
        return copy

    c_saved = local(saved.at[0], tok.at[0], 0)
    c_acts = local(acts.at[0], tok.at[1], 1)
    c_grads = local(grads.at[0], tok.at[2], 2)
    c_win = local(w_in.at[0], win.at[0], 3)
    c_wout = local(w_out.at[0], wout.at[0], 4)

    partners = [chip(0, 1), chip(0, -1), chip(1, 0), chip(-1, 0), plane(1), plane(-1), sibling]
    barrier = pltpu.get_barrier_semaphore()
    for dev in partners:
        pl.semaphore_signal(barrier, inc=1, device_id=dev, device_id_type=MESH)
    pl.semaphore_wait(barrier, len(partners))

    x_acts = send(acts.at[0], tok.at[3], ex_send.at[0], ex_recv.at[0], plane(1))
    x_grads = send(grads.at[0], tok.at[4], ex_send.at[1], ex_recv.at[1], plane(-1))
    x_win = send(w_in.at[0], win.at[1], ex_send.at[2], ex_recv.at[2], sibling)
    x_wout = send(w_out.at[0], wout.at[1], ex_send.at[3], ex_recv.at[3], sibling)

    def cols(h, part_no=None):
        if part_no is None:
            return pl.ds(h * H, H)
        return pl.ds(h * H + part_no * Q, Q)

    def first(h, d):
        return (0, d) if h == 0 else (d, 0)

    def second(h, d):
        return (d, 0) if h == 0 else (0, d)

    def slot(h, df, ds):
        return at(ds, df) if h == 0 else at(df, ds)

    msgs = {}

    def ag_send_msg(k, h, m, df, ds, sub, dev):
        yy, xx = slot(h, df, ds)
        ref = ag.at[k, yy, xx, :, cols(h, sub)]
        msgs[k, h, m] = send(ref, ref, ag_send.at[k, h, m], ag_recv.at[k, h, m], chip(*dev))

    J = (0, -1, 1, 2)

    def ag0(k, h):
        ag_send_msg(k, h, 0, 0, 0, None, first(h, 1))
        ag_send_msg(k, h, 1, 0, 0, None, first(h, -1))
        ag_send_msg(k, h, 4, 0, 0, None, second(h, 1))
        ag_send_msg(k, h, 5, 0, 0, None, second(h, -1))

    def ag1(k, h):
        for m, d in ((0, -1), (1, 1)):
            msgs[k, h, m].wait_recv()
            ag_send_msg(k, h, 2 + m, d, 0, m, first(h, -d))
            j = J.index(d)
            ag_send_msg(k, h, 4 + 2 * j, d, 0, None, second(h, 1))
            ag_send_msg(k, h, 5 + 2 * j, d, 0, None, second(h, -1))

    def ag_forward(k, h, j):
        for m, d in ((0, -1), (1, 1)):
            msgs[k, h, 4 + 2 * j + m].wait_recv()
            ag_send_msg(k, h, 12 + 2 * j + m, J[j], d, m, second(h, -d))

    def ag2(k, h):
        ag_forward(k, h, 0)

    def ag3(k, h):
        msgs[k, h, 2].wait_recv()
        msgs[k, h, 3].wait_recv()
        ag_send_msg(k, h, 10, 2, 0, None, second(h, 1))
        ag_send_msg(k, h, 11, 2, 0, None, second(h, -1))

    def ag4(k, h):
        ag_forward(k, h, 1)
        ag_forward(k, h, 2)

    def ag5(k, h):
        ag_forward(k, h, 3)

    def ag6(k, h):
        for m in range(12, 20):
            msgs[k, h, m].wait_recv()

    ag_stages = (ag0, ag1, ag2, ag3, ag4, ag5, ag6)

    def gather(k, stage):
        for h in range(2):
            ag_stages[stage](k, h)

    def row(ref, h, d, csl):
        if h == 0:
            return ref.at[at(d, 0)[0], :, :, csl]
        return ref.at[:, at(0, d)[1], :, csl]

    rmsgs = {}

    def rs_send_msg(r, h, m, src, dst, dev):
        rmsgs[r, h, m] = send(src, dst, rs_send.at[r, h, m], rs_recv.at[r, h, m], chip(*dev))

    def rs0(r, h):
        p = part.at[r]
        for m, d in ((0, 1), (1, -1)):
            rs_send_msg(r, h, m, row(p, h, 2, cols(h, m)), r1.at[r, h, m], second(h, d))
        for m, d in ((0, 1), (1, -1)):
            rs_send_msg(
                r, h, 2 + m, row(p, h, d, cols(h, 1 - m)), r2.at[r, h, m, :, :, pl.ds((1 - m) * Q, Q)], second(h, d)
            )

    def rs1(r, h):
        p = part.at[r]
        for m, d in ((0, 1), (1, -1)):
            rmsgs[r, h, m].wait_recv()
            near = row(p, h, d, cols(h, m))
            near[...] = (near[...].astype(F32) + r1[r, h, m].astype(F32)).astype(BF16)
            rs_send_msg(r, h, 4 + m, near, r2.at[r, h, m, :, :, pl.ds(m * Q, Q)], second(h, d))

    def rs2(r, h):
        p = part.at[r]
        for m in range(2, 6):
            rmsgs[r, h, m].wait_recv()
        own = row(p, h, 0, cols(h))
        q[r, h] = (own[...].astype(F32) + r2[r, h, 0].astype(F32) + r2[r, h, 1].astype(F32)).astype(BF16)

        def place(d):
            return at(0, d)[1] if h == 0 else at(d, 0)[0]

        for m, d in ((0, 1), (1, -1)):
            rs_send_msg(
                r, h, 6 + m, q.at[r, h, place(2), :, pl.ds(m * Q, Q)], r3.at[r, h, m], first(h, d)
            )
        for m, d in ((0, 1), (1, -1)):
            rs_send_msg(
                r, h, 8 + m, q.at[r, h, place(d), :, pl.ds((1 - m) * Q, Q)],
                r4.at[r, h, m, :, pl.ds((1 - m) * Q, Q)], first(h, d),
            )

    def rs3(r, h):
        def place(d):
            return at(0, d)[1] if h == 0 else at(d, 0)[0]

        for m, d in ((0, 1), (1, -1)):
            rmsgs[r, h, 6 + m].wait_recv()
            near = q.at[r, h, place(d), :, pl.ds(m * Q, Q)]
            near[...] = (near[...].astype(F32) + r3[r, h, m].astype(F32)).astype(BF16)
            rs_send_msg(r, h, 10 + m, near, r4.at[r, h, m, :, pl.ds(m * Q, Q)], first(h, d))

    def rs4(r, h):
        for m in range(8, 12):
            rmsgs[r, h, m].wait_recv()
        place = x if h == 0 else y
        return q[r, h, place].astype(F32) + r4[r, h, 0].astype(F32) + r4[r, h, 1].astype(F32)

    rs_stages = (rs0, rs1, rs2, rs3)

    def scatter(r, stage):
        for h in range(2):
            rs_stages[stage](r, h)

    def rows(k):
        return ag[k].reshape(tokens, D)

    c_saved.wait()
    kept = tok[0].astype(F32)
    ag[NB, y, x] = (kept * inv_rms(kept)).astype(BF16)
    gather(NB, 0)
    c_acts.wait()
    c_grads.wait()
    x_grads.wait_recv()
    ag[CT, y, x] = jnp.where(z == n_z - 1, tok[2], tok[4])
    x_acts.wait_recv()
    tok[1] = jnp.where(z == 0, tok[1], tok[3])
    inputs = tok[1].astype(F32)
    ag[NF, y, x] = (inputs * inv_rms(inputs)).astype(BF16)
    gather(NB, 1)
    gather(NB, 2)
    gather(NB, 3)
    gather(CT, 0)
    gather(NB, 4)
    gather(CT, 1)
    gather(NB, 5)
    gather(CT, 2)
    gather(CT, 3)
    gather(NB, 6)
    gather(NF, 0)
    gather(CT, 4)
    c_win.wait()
    x_win.wait_recv()
    for c in range(2):
        value, grad = gelu_and_slope(nn(rows(NB), win[c]))
        hid[c] = value.astype(BF16)
        slope[c] = grad
    gather(NF, 1)
    gather(CT, 5)
    gather(NF, 2)
    gather(NF, 3)
    gather(CT, 6)
    gather(NF, 4)
    c_wout.wait()
    x_wout.wait_recv()
    for c in range(2):
        dpre[c] = (nt(rows(CT), wout[c]) * slope[c]).astype(BF16)
    gather(NF, 5)
    for h in range(2):
        for s in range(2):
            csl = cols(h, s)
            part[BWD, :, :, :, csl] = (
                (nt(dpre[0], win[0, csl, :]) + nt(dpre[1], win[1, csl, :])).astype(BF16).reshape(4, 4, 16, Q)
            )
        rs0(BWD, h)
    gather(NF, 6)
    for c in range(2):
        hid_f = gelu(nn(rows(NF), win[c])).astype(BF16)
        slope[c] = hid_f.astype(F32)
    scatter(BWD, 1)
    for h in range(2):
        for s in range(2):
            csl = cols(h, s)
            part[FWD, :, :, :, csl] = (
                (nn(slope[0].astype(BF16), wout[0, :, csl]) + nn(slope[1].astype(BF16), wout[1, :, csl]))
                .astype(BF16).reshape(4, 4, 16, Q)
            )
        rs0(FWD, h)
    scatter(BWD, 2)
    gin_s[...] = tn(rows(NB), dpre[1]).astype(BF16)
    x_gin = send(gin_s, gin_r, ex_send.at[4], ex_recv.at[4], sibling)
    scatter(BWD, 3)
    scatter(FWD, 1)
    gout_s[...] = tn(hid[1], rows(CT)).astype(BF16)
    x_gout = send(gout_s, gout_r, ex_send.at[5], ex_recv.at[5], sibling)
    scatter(FWD, 2)
    gin_o[...] = tn(rows(NB), dpre[0]).astype(BF16)
    gout_o[...] = tn(hid[0], rows(CT)).astype(BF16)
    scatter(FWD, 3)
    x_gin.wait_recv()
    gin_o[...] = (gin_o[...].astype(F32) + gin_r[...].astype(F32)).astype(BF16)
    out_gin = pltpu.make_async_copy(gin_o, o_gin.at[0], loc_sem.at[5])
    out_gin.start()
    x_gout.wait_recv()
    gout_o[...] = (gout_o[...].astype(F32) + gout_r[...].astype(F32)).astype(BF16)
    out_gout = pltpu.make_async_copy(gout_o, o_gout.at[0], loc_sem.at[6])
    out_gout.start()

    d_normed = jnp.concatenate([rs4(BWD, 0), rs4(BWD, 1)], axis=-1)
    kept = tok[0].astype(F32)
    scale = inv_rms(kept)
    inner = jnp.mean(d_normed * kept, axis=-1, keepdims=True)
    back = scale * d_normed - kept * (scale * scale * scale * inner)
    o_grads[0] = (ag[CT, y, x].astype(F32) + back).astype(BF16)
    o_acts[0] = (tok[1].astype(F32) + jnp.concatenate([rs4(FWD, 0), rs4(FWD, 1)], axis=-1)).astype(BF16)
    out_gin.wait()
    out_gout.wait()
    for copy in sent:
        copy.wait_send()


def shards(n_z, acts, grads, saved, w_in, w_out):
    _, T, D = acts.shape
    U = w_in.shape[2]
    H, Q = D // 2, D // 4
    vmem = pltpu.VMEM
    sem = pltpu.SemaphoreType.DMA
    anywhere = pl.BlockSpec(memory_space=pl.ANY)
    whole = pl.BlockSpec(memory_space=pltpu.VMEM)
    tokens = 16 * T
    return pl.pallas_call(
        functools.partial(kernel, n_z),
        out_shape=(
            jax.ShapeDtypeStruct(acts.shape, BF16),
            jax.ShapeDtypeStruct(acts.shape, BF16),
            jax.ShapeDtypeStruct(w_in.shape, BF16),
            jax.ShapeDtypeStruct(w_out.shape, BF16),
        ),
        in_specs=[anywhere] * 5,
        out_specs=(whole, whole, anywhere, anywhere),
        scratch_shapes=[
            vmem((5, T, D), BF16),
            vmem((3, 4, 4, T, D), BF16),
            vmem((2, D, U), BF16),
            vmem((2, U, D), BF16),
            vmem((2, 4, 4, T, D), BF16),
            vmem((2, 2, 2, 4, T, Q), BF16),
            vmem((2, 2, 2, 4, T, H), BF16),
            vmem((2, 2, 2, T, Q), BF16),
            vmem((2, 2, 2, T, H), BF16),
            vmem((2, 2, 4, T, H), BF16),
            vmem((2, tokens, U), BF16),
            vmem((2, tokens, U), BF16),
            vmem((2, tokens, U), F32),
            vmem((D, U), BF16),
            vmem((D, U), BF16),
            vmem((U, D), BF16),
            vmem((U, D), BF16),
            vmem((D, U), BF16),
            vmem((U, D), BF16),
            sem((7,)),
            sem((3, 2, 20)),
            sem((3, 2, 20)),
            sem((2, 2, 12)),
            sem((2, 2, 12)),
            sem((6,)),
            sem((6,)),
        ],
        compiler_params=pltpu.CompilerParams(
            collective_id=0, has_side_effects=True, vmem_limit_bytes=56 * 1024 * 1024
        ),
    )(acts, grads, saved, w_in, w_out)


def solution(mesh):
    rows_split = P("section", ("tensor", "dp"), None)
    columns_split = P("section", None, ("tensor", "dp"))
    return jax.shard_map(
        functools.partial(shards, mesh.shape["section"] // 2),
        mesh=mesh,
        in_specs=(rows_split, rows_split, rows_split, columns_split, rows_split),
        out_specs=(rows_split, rows_split, columns_split, rows_split),
        check_vma=False,
    )
```

```python
import functools

import jax
import jax.numpy as jnp
from jax import lax
from jax.experimental import pallas as pl
from jax.experimental.pallas import tpu as pltpu
from jax.sharding import PartitionSpec as P

MESH = pl.DeviceIdType.MESH
F32, BF16 = jnp.float32, jnp.bfloat16
EPS = 1e-05
NB, CT, NF = 0, 1, 2
BWD, FWD = 0, 1
GELU_A, GELU_B = 0.7978845608028654, 0.044715


def inv_rms(values):
    return lax.rsqrt(jnp.mean(values * values, axis=-1, keepdims=True) + EPS)


def gelu(v):
    return 0.5 * v * (1.0 + jnp.tanh(GELU_A * (v + GELU_B * (v * v * v))))


def gelu_and_slope(v):
    square = v * v
    t = jnp.tanh(GELU_A * (v + GELU_B * (v * square)))
    value = 0.5 * v * (1.0 + t)
    slope = 0.5 * (1.0 + t) + 0.5 * v * (1.0 - t * t) * (GELU_A * (1.0 + 3.0 * GELU_B * square))
    return value, slope


def nn(a, b):
    return jnp.dot(a, b, preferred_element_type=F32)


def nt(a, b):
    return lax.dot_general(a, b, (((1,), (1,)), ((), ())), preferred_element_type=F32)


def tn(a, b):
    return lax.dot_general(a, b, (((0,), (0,)), ((), ())), preferred_element_type=F32)


def kernel(
    n_z, acts, grads, saved, w_in, w_out, o_acts, o_grads, o_gin, o_gout,
    tok, ag, win, wout, part, r1, r2, r3, r4, q, hid, fwd_hid, dpre, slope, gin_s, gin_r, gout_s, gout_r,
    loc_sem, ag_send, ag_recv, rs_send, rs_recv, ex_send, ex_recv,
):
    sec, y, dp = lax.axis_index("section"), lax.axis_index("tensor"), lax.axis_index("dp")
    z = lax.rem(sec, n_z)
    x_hi = sec // n_z
    x = 2 * x_hi + dp // 2
    core = lax.rem(dp, 2)
    D = ag.shape[-1]
    H, Q = D // 2, D // 4
    tokens = 16 * ag.shape[3]

    def at(dy, dx):
        return lax.rem(y + dy + 4, 4), lax.rem(x + dx + 4, 4)

    def chip(dy, dx):
        yy, xx = at(dy, dx)
        return ((xx // 2) * n_z + z, yy, 2 * lax.rem(xx, 2) + core)

    def plane(dz):
        return (x_hi * n_z + lax.rem(z + dz + n_z, n_z), y, dp)

    sibling = (sec, y, dp + 1 - 2 * core)

    sent = []

    def send(src, dst, ssem, rsem, dev):
        copy = pltpu.make_async_remote_copy(
            src_ref=src, dst_ref=dst, send_sem=ssem, recv_sem=rsem, device_id=dev, device_id_type=MESH
        )
        copy.start()
        sent.append(copy)
        return copy

    def local(src, dst, i):
        copy = pltpu.make_async_copy(src, dst, loc_sem.at[i])
        copy.start()
        return copy

    c_saved = local(saved.at[0], tok.at[0], 0)
    c_acts = local(acts.at[0], tok.at[1], 1)
    c_grads = local(grads.at[0], tok.at[2], 2)
    c_win = local(w_in.at[0], win.at[0], 3)
    c_wout = local(w_out.at[0], wout.at[0], 4)

    partners = [chip(0, 1), chip(0, -1), chip(1, 0), chip(-1, 0), plane(1), plane(-1), sibling]
    barrier = pltpu.get_barrier_semaphore()
    for dev in partners:
        pl.semaphore_signal(barrier, inc=1, device_id=dev, device_id_type=MESH)
    pl.semaphore_wait(barrier, len(partners))

    x_acts = send(acts.at[0], tok.at[3], ex_send.at[0], ex_recv.at[0], plane(1))
    x_grads = send(grads.at[0], tok.at[4], ex_send.at[1], ex_recv.at[1], plane(-1))
    def cols(h, part_no=None):
        if part_no is None:
            return pl.ds(h * H, H)
        return pl.ds(h * H + part_no * Q, Q)

    def first(h, d):
        return (0, d) if h == 0 else (d, 0)

    def second(h, d):
        return (d, 0) if h == 0 else (0, d)

    def slot(h, df, ds):
        return at(ds, df) if h == 0 else at(df, ds)

    msgs = {}

    def ag_send_msg(k, h, m, df, ds, sub, dev):
        yy, xx = slot(h, df, ds)
        ref = ag.at[k, yy, xx, :, cols(h, sub)]
        msgs[k, h, m] = send(ref, ref, ag_send.at[k, h, m], ag_recv.at[k, h, m], chip(*dev))

    J = (0, -1, 1, 2)

    def ag0(k, h):
        ag_send_msg(k, h, 0, 0, 0, None, first(h, 1))
        ag_send_msg(k, h, 1, 0, 0, None, first(h, -1))
        ag_send_msg(k, h, 4, 0, 0, None, second(h, 1))
        ag_send_msg(k, h, 5, 0, 0, None, second(h, -1))

    def ag1(k, h):
        for m, d in ((0, -1), (1, 1)):
            msgs[k, h, m].wait_recv()
            ag_send_msg(k, h, 2 + m, d, 0, m, first(h, -d))
            j = J.index(d)
            ag_send_msg(k, h, 4 + 2 * j, d, 0, None, second(h, 1))
            ag_send_msg(k, h, 5 + 2 * j, d, 0, None, second(h, -1))

    def ag_forward(k, h, j):
        for m, d in ((0, -1), (1, 1)):
            msgs[k, h, 4 + 2 * j + m].wait_recv()
            ag_send_msg(k, h, 12 + 2 * j + m, J[j], d, m, second(h, -d))

    def ag2(k, h):
        ag_forward(k, h, 0)

    def ag3(k, h):
        msgs[k, h, 2].wait_recv()
        msgs[k, h, 3].wait_recv()
        ag_send_msg(k, h, 10, 2, 0, None, second(h, 1))
        ag_send_msg(k, h, 11, 2, 0, None, second(h, -1))

    def ag4(k, h):
        ag_forward(k, h, 1)
        ag_forward(k, h, 2)

    def ag5(k, h):
        ag_forward(k, h, 3)

    def ag6(k, h):
        for m in range(12, 20):
            msgs[k, h, m].wait_recv()

    ag_stages = (ag0, ag1, ag2, ag3, ag4, ag5, ag6)

    def gather(k, stage):
        for h in range(2):
            ag_stages[stage](k, h)

    def row(ref, h, d, csl):
        if h == 0:
            return ref.at[at(d, 0)[0], :, :, csl]
        return ref.at[:, at(0, d)[1], :, csl]

    rmsgs = {}

    def rs_send_msg(r, h, m, src, dst, dev):
        rmsgs[r, h, m] = send(src, dst, rs_send.at[r, h, m], rs_recv.at[r, h, m], chip(*dev))

    def rs0(r, h):
        p = part.at[r]
        for m, d in ((0, 1), (1, -1)):
            rs_send_msg(r, h, m, row(p, h, 2, cols(h, m)), r1.at[r, h, m], second(h, d))
        for m, d in ((0, 1), (1, -1)):
            rs_send_msg(
                r, h, 2 + m, row(p, h, d, cols(h, 1 - m)), r2.at[r, h, m, :, :, pl.ds((1 - m) * Q, Q)], second(h, d)
            )

    def rs1(r, h):
        p = part.at[r]
        for m, d in ((0, 1), (1, -1)):
            rmsgs[r, h, m].wait_recv()
            near = row(p, h, d, cols(h, m))
            near[...] = (near[...].astype(F32) + r1[r, h, m].astype(F32)).astype(BF16)
            rs_send_msg(r, h, 4 + m, near, r2.at[r, h, m, :, :, pl.ds(m * Q, Q)], second(h, d))

    def rs2(r, h):
        p = part.at[r]
        for m in range(2, 6):
            rmsgs[r, h, m].wait_recv()
        own = row(p, h, 0, cols(h))
        q[r, h] = (own[...].astype(F32) + r2[r, h, 0].astype(F32) + r2[r, h, 1].astype(F32)).astype(BF16)

        def place(d):
            return at(0, d)[1] if h == 0 else at(d, 0)[0]

        for m, d in ((0, 1), (1, -1)):
            rs_send_msg(
                r, h, 6 + m, q.at[r, h, place(2), :, pl.ds(m * Q, Q)], r3.at[r, h, m], first(h, d)
            )
        for m, d in ((0, 1), (1, -1)):
            rs_send_msg(
                r, h, 8 + m, q.at[r, h, place(d), :, pl.ds((1 - m) * Q, Q)],
                r4.at[r, h, m, :, pl.ds((1 - m) * Q, Q)], first(h, d),
            )

    def rs3(r, h):
        def place(d):
            return at(0, d)[1] if h == 0 else at(d, 0)[0]

        for m, d in ((0, 1), (1, -1)):
            rmsgs[r, h, 6 + m].wait_recv()
            near = q.at[r, h, place(d), :, pl.ds(m * Q, Q)]
            near[...] = (near[...].astype(F32) + r3[r, h, m].astype(F32)).astype(BF16)
            rs_send_msg(r, h, 10 + m, near, r4.at[r, h, m, :, pl.ds(m * Q, Q)], first(h, d))

    def rs4(r, h):
        for m in range(8, 12):
            rmsgs[r, h, m].wait_recv()
        place = x if h == 0 else y
        return q[r, h, place].astype(F32) + r4[r, h, 0].astype(F32) + r4[r, h, 1].astype(F32)

    rs_stages = (rs0, rs1, rs2, rs3)

    def scatter(r, stage):
        for h in range(2):
            rs_stages[stage](r, h)

    def rows(k):
        return ag[k].reshape(tokens, D)

    def prep_nb():
        c_saved.wait()
        kept = tok[0].astype(F32)
        ag[NB, y, x] = (kept * inv_rms(kept)).astype(BF16)

    def prep_ct():
        c_grads.wait()
        x_grads.wait_recv()
        ag[CT, y, x] = jnp.where(z == n_z - 1, tok[2], tok[4])

    def prep_nf():
        c_acts.wait()
        x_acts.wait_recv()
        tok[1] = jnp.where(z == 0, tok[1], tok[3])
        inputs = tok[1].astype(F32)
        ag[NF, y, x] = (inputs * inv_rms(inputs)).astype(BF16)

    def make_pre():
        c_win.wait()
        exchange[2].wait_recv()
        for c in range(2):
            value, grad = gelu_and_slope(nt(rows(NB), win[c]))
            hid[c] = value.astype(BF16)
            slope[c] = grad

    def make_dpre():
        c_wout.wait()
        exchange[3].wait_recv()
        for c in range(2):
            dpre[c] = (nt(rows(CT), wout[c]) * slope[c]).astype(BF16)

    def make_bwd(h):
        for s in range(2):
            csl = cols(h, s)
            part[BWD, :, :, :, csl] = (
                (nn(dpre[0], win[0, :, csl]) + nn(dpre[1], win[1, :, csl])).astype(BF16).reshape(4, 4, 16, Q)
            )
        rs0(BWD, h)

    def make_hidden():
        for c in range(2):
            fwd_hid[c] = gelu(nt(rows(NF), win[c])).astype(BF16)

    def make_fwd(h):
        for s in range(2):
            csl = cols(h, s)
            part[FWD, :, :, :, csl] = (
                (nn(fwd_hid[0], wout[0, :, csl]) + nn(fwd_hid[1], wout[1, :, csl])).astype(BF16).reshape(4, 4, 16, Q)
            )
        rs0(FWD, h)

    def give_gin():
        gin_s[...] = tn(dpre[1], rows(NB)).astype(BF16)
        exchange[4] = send(gin_s, gin_r, ex_send.at[4], ex_recv.at[4], sibling)

    def give_gout():
        gout_s[...] = tn(hid[1], rows(CT)).astype(BF16)
        exchange[5] = send(gout_s, gout_r, ex_send.at[5], ex_recv.at[5], sibling)

    def keep_grads():
        o_gin[0] = tn(dpre[0], rows(NB)).astype(BF16)
        o_gout[0] = tn(hid[0], rows(CT)).astype(BF16)

    def add_grads():
        exchange[4].wait_recv()
        o_gin[0] = (o_gin[0].astype(F32) + gin_r[...].astype(F32)).astype(BF16)
        exchange[5].wait_recv()
        o_gout[0] = (o_gout[0].astype(F32) + gout_r[...].astype(F32)).astype(BF16)

    exchange = {}

    def meet_sibling():
        exchange[2] = send(w_in.at[0], win.at[1], ex_send.at[2], ex_recv.at[2], sibling)
        exchange[3] = send(w_out.at[0], wout.at[1], ex_send.at[3], ex_recv.at[3], sibling)

    def finish_bwd():
        d_normed = jnp.concatenate([rs4(BWD, 0), rs4(BWD, 1)], axis=-1)
        kept = tok[0].astype(F32)
        scale = inv_rms(kept)
        inner = jnp.mean(d_normed * kept, axis=-1, keepdims=True)
        back = scale * d_normed - kept * (scale * scale * scale * inner)
        o_grads[0] = (ag[CT, y, x].astype(F32) + back).astype(BF16)

    def finish_fwd():
        o_acts[0] = (tok[1].astype(F32) + jnp.concatenate([rs4(FWD, 0), rs4(FWD, 1)], axis=-1)).astype(BF16)

    prep_nb()
    gather(NB, 0)
    meet_sibling()
    prep_ct()
    gather(CT, 0)
    prep_nf()
    gather(NF, 0)
    gather(NB, 1)
    gather(CT, 1)
    gather(NF, 1)
    gather(NB, 2)
    gather(CT, 2)
    gather(NF, 2)
    gather(NB, 3)
    gather(CT, 3)
    gather(NF, 3)
    gather(NB, 4)
    gather(CT, 4)
    gather(NF, 4)
    gather(NB, 5)
    gather(CT, 5)
    gather(NF, 5)
    gather(NB, 6)
    make_pre()
    gather(CT, 6)
    make_dpre()
    make_bwd(0)
    make_bwd(1)
    gather(NF, 6)
    make_hidden()
    make_fwd(0)
    make_fwd(1)
    scatter(BWD, 1)
    scatter(FWD, 1)
    give_gin()
    scatter(BWD, 2)
    give_gout()
    scatter(FWD, 2)
    scatter(BWD, 3)
    scatter(FWD, 3)
    keep_grads()
    finish_bwd()
    finish_fwd()
    add_grads()
    for copy in sent:
        copy.wait_send()


def store(*refs):
    copies = [pltpu.make_async_copy(refs[i], refs[4 + i], refs[8].at[i]) for i in range(4)]
    for copy in copies:
        copy.start()
    for copy in copies:
        copy.wait()


def shards(n_z, acts, grads, saved, w_in, w_out):
    _, T, D = acts.shape
    w_in = jnp.swapaxes(w_in, 1, 2)
    U = w_in.shape[1]
    H, Q = D // 2, D // 4
    vmem = pltpu.VMEM
    sem = pltpu.SemaphoreType.DMA
    anywhere = pl.BlockSpec(memory_space=pl.ANY)
    whole = pl.BlockSpec(memory_space=pltpu.VMEM)
    tokens = 16 * T
    results = pl.pallas_call(
        functools.partial(kernel, n_z),
        out_shape=(
            vmem(acts.shape, BF16),
            vmem(acts.shape, BF16),
            vmem(w_in.shape, BF16),
            vmem(w_out.shape, BF16),
        ),
        in_specs=[anywhere] * 5,
        out_specs=(whole,) * 4,
        scratch_shapes=[
            vmem((5, T, D), BF16),
            vmem((3, 4, 4, T, D), BF16),
            vmem((2, U, D), BF16),
            vmem((2, U, D), BF16),
            vmem((2, 4, 4, T, D), BF16),
            vmem((2, 2, 2, 4, T, Q), BF16),
            vmem((2, 2, 2, 4, T, H), BF16),
            vmem((2, 2, 2, T, Q), BF16),
            vmem((2, 2, 2, T, H), BF16),
            vmem((2, 2, 4, T, H), BF16),
            vmem((2, tokens, U), BF16),
            vmem((2, tokens, U), BF16),
            vmem((2, tokens, U), BF16),
            vmem((2, tokens, U), F32),
            vmem((U, D), BF16),
            vmem((U, D), BF16),
            vmem((U, D), BF16),
            vmem((U, D), BF16),
            sem((5,)),
            sem((3, 2, 20)),
            sem((3, 2, 20)),
            sem((2, 2, 12)),
            sem((2, 2, 12)),
            sem((6,)),
            sem((6,)),
        ],
        compiler_params=pltpu.CompilerParams(
            collective_id=0, has_side_effects=True, vmem_limit_bytes=56 * 1024 * 1024
        ),
    )(acts, grads, saved, w_in, w_out)
    out_acts, out_grads, grad_in, grad_out = pl.pallas_call(
        store,
        out_shape=tuple(jax.ShapeDtypeStruct(r.shape, r.dtype) for r in results),
        in_specs=[anywhere] * 4,
        out_specs=(anywhere,) * 4,
        scratch_shapes=[sem((4,))],
        compiler_params=pltpu.CompilerParams(vmem_limit_bytes=1024 * 1024),
    )(*results)
    return out_acts, out_grads, jnp.swapaxes(grad_in, 1, 2), grad_out


def solution(mesh):
    rows_split = P("section", ("tensor", "dp"), None)
    columns_split = P("section", None, ("tensor", "dp"))
    return jax.shard_map(
        functools.partial(shards, mesh.shape["section"] // 2),
        mesh=mesh,
        in_specs=(rows_split, rows_split, rows_split, columns_split, rows_split),
        out_specs=(rows_split, rows_split, columns_split, rows_split),
        check_vma=False,
    )
```

```python
import functools

import jax
import jax.numpy as jnp
from jax import lax
from jax.experimental import pallas as pl
from jax.experimental.pallas import tpu as pltpu
from jax.sharding import PartitionSpec as P

MESH = pl.DeviceIdType.MESH
F32, BF16 = jnp.float32, jnp.bfloat16
EPS = 1e-05
NB, CT, NF = 0, 1, 2
BWD, FWD = 0, 1
GELU_A, GELU_B = 0.7978845608028654, 0.044715


def inv_rms(values):
    return lax.rsqrt(jnp.mean(values * values, axis=-1, keepdims=True) + EPS)


def gelu(v):
    return 0.5 * v * (1.0 + jnp.tanh(GELU_A * (v + GELU_B * (v * v * v))))


def gelu_and_slope(v):
    square = v * v
    t = jnp.tanh(GELU_A * (v + GELU_B * (v * square)))
    value = 0.5 * v * (1.0 + t)
    slope = 0.5 * (1.0 + t) + 0.5 * v * (1.0 - t * t) * (GELU_A * (1.0 + 3.0 * GELU_B * square))
    return value, slope


def nn(a, b):
    return jnp.dot(a, b, preferred_element_type=F32)


def nt(a, b):
    return lax.dot_general(a, b, (((1,), (1,)), ((), ())), preferred_element_type=F32)


def tn(a, b):
    return lax.dot_general(a, b, (((0,), (0,)), ((), ())), preferred_element_type=F32)


def kernel(
    n_z, acts, grads, saved, w_in, w_out, o_acts, o_grads, o_gin, o_gout,
    tok, ag, win, wout, part, r1, r2, r4, q, hid, fwd_hid, dpre, slope, gin_s, gin_r, gout_s, gout_r,
    loc_sem, ag_send, ag_recv, rs_send, rs_recv, ex_send, ex_recv,
):
    sec, y, dp = lax.axis_index("section"), lax.axis_index("tensor"), lax.axis_index("dp")
    z = lax.rem(sec, n_z)
    x_hi = sec // n_z
    x = 2 * x_hi + dp // 2
    core = lax.rem(dp, 2)
    D = ag.shape[-1]
    H, Q = D // 2, D // 4
    tokens = 16 * ag.shape[3]

    def at(dy, dx):
        return lax.rem(y + dy + 4, 4), lax.rem(x + dx + 4, 4)

    def chip(dy, dx):
        yy, xx = at(dy, dx)
        return ((xx // 2) * n_z + z, yy, 2 * lax.rem(xx, 2) + core)

    def plane(dz):
        return (sec + dz, y, dp)

    sibling = (sec, y, dp + 1 - 2 * core)

    sent = []

    def send(src, dst, ssem, rsem, dev):
        copy = pltpu.make_async_remote_copy(
            src_ref=src, dst_ref=dst, send_sem=ssem, recv_sem=rsem, device_id=dev, device_id_type=MESH
        )
        copy.start()
        sent.append(copy)
        return copy

    def local(src, dst, i):
        copy = pltpu.make_async_copy(src, dst, loc_sem.at[i])
        copy.start()
        return copy

    c_saved = local(saved.at[0], tok.at[0], 0)
    c_acts = local(acts.at[0], tok.at[1], 1)
    c_grads = local(grads.at[0], tok.at[2], 2)
    c_win = local(w_in.at[0], win.at[0], 3)
    c_wout = local(w_out.at[0], wout.at[0], 4)

    has_next, has_last = z < n_z - 1, z > 0
    barrier = pltpu.get_barrier_semaphore()

    def greet(dev):
        pl.semaphore_signal(barrier, inc=1, device_id=dev, device_id_type=MESH)

    pl.when(has_next)(lambda: greet(plane(1)))
    pl.when(has_last)(lambda: greet(plane(-1)))
    for dev in (chip(0, 1), chip(0, -1), chip(1, 0), chip(-1, 0), sibling):
        greet(dev)
    pl.semaphore_wait(barrier, 5 + jnp.where(has_next, 1, 0) + jnp.where(has_last, 1, 0))

    def shifted(src, dst, n, dev):
        return pltpu.make_async_remote_copy(
            src_ref=src, dst_ref=dst, send_sem=ex_send.at[n], recv_sem=ex_recv.at[n], device_id=dev,
            device_id_type=MESH,
        )

    x_acts = shifted(acts.at[0], tok.at[3], 0, plane(1))
    x_grads = shifted(grads.at[0], tok.at[4], 1, plane(-1))
    pl.when(has_next)(x_acts.start)
    pl.when(has_last)(x_grads.start)

    def cols(h, part_no=None):
        if part_no is None:
            return pl.ds(h * H, H)
        return pl.ds(h * H + part_no * Q, Q)

    def first(h, d):
        return (0, d) if h == 0 else (d, 0)

    def second(h, d):
        return (d, 0) if h == 0 else (0, d)

    def slot(h, df, ds):
        return at(ds, df) if h == 0 else at(df, ds)

    msgs = {}

    def ag_send_msg(k, h, m, df, ds, sub, dev):
        yy, xx = slot(h, df, ds)
        ref = ag.at[k, yy, xx, :, cols(h, sub)]
        msgs[k, h, m] = send(ref, ref, ag_send.at[k, h, m], ag_recv.at[k, h, m], chip(*dev))

    J = (0, -1, 1, 2)

    def ag0(k, h):
        ag_send_msg(k, h, 0, 0, 0, None, first(h, 1))
        ag_send_msg(k, h, 1, 0, 0, None, first(h, -1))
        ag_send_msg(k, h, 4, 0, 0, None, second(h, 1))
        ag_send_msg(k, h, 5, 0, 0, None, second(h, -1))

    def ag1(k, h):
        for m, d in ((0, -1), (1, 1)):
            msgs[k, h, m].wait_recv()
            ag_send_msg(k, h, 2 + m, d, 0, m, first(h, -d))
            j = J.index(d)
            ag_send_msg(k, h, 4 + 2 * j, d, 0, None, second(h, 1))
            ag_send_msg(k, h, 5 + 2 * j, d, 0, None, second(h, -1))

    def ag_forward(k, h, j):
        for m, d in ((0, -1), (1, 1)):
            msgs[k, h, 4 + 2 * j + m].wait_recv()
            ag_send_msg(k, h, 12 + 2 * j + m, J[j], d, m, second(h, -d))

    def ag2(k, h):
        ag_forward(k, h, 0)

    def ag3(k, h):
        msgs[k, h, 2].wait_recv()
        msgs[k, h, 3].wait_recv()
        ag_send_msg(k, h, 10, 2, 0, None, second(h, 1))
        ag_send_msg(k, h, 11, 2, 0, None, second(h, -1))

    def ag4(k, h):
        ag_forward(k, h, 1)
        ag_forward(k, h, 2)

    def ag5(k, h):
        ag_forward(k, h, 3)

    def ag6(k, h):
        for m in range(12, 20):
            msgs[k, h, m].wait_recv()

    ag_stages = (ag0, ag1, ag2, ag3, ag4, ag5, ag6)

    def gather(k, stage):
        for h in range(2):
            ag_stages[stage](k, h)

    def row(ref, h, d, csl):
        if h == 0:
            return ref.at[at(d, 0)[0], :, :, csl]
        return ref.at[:, at(0, d)[1], :, csl]

    rmsgs = {}

    def rs_send_msg(r, h, m, src, dst, dev):
        rmsgs[r, h, m] = send(src, dst, rs_send.at[r, h, m], rs_recv.at[r, h, m], chip(*dev))

    def rs0(r, h):
        p = part.at[r]
        for m, d in ((0, 1), (1, -1)):
            rs_send_msg(r, h, m, row(p, h, 2, cols(h, m)), r1.at[r, h, m], second(h, d))
        for m, d in ((0, 1), (1, -1)):
            rs_send_msg(
                r, h, 2 + m, row(p, h, d, cols(h, 1 - m)), r2.at[r, h, m, :, :, pl.ds((1 - m) * Q, Q)], second(h, d)
            )

    def rs1(r, h):
        p = part.at[r]
        for m, d in ((0, 1), (1, -1)):
            rmsgs[r, h, m].wait_recv()
            near = row(p, h, d, cols(h, m))
            near[...] = (near[...].astype(F32) + r1[r, h, m].astype(F32)).astype(BF16)
            rs_send_msg(r, h, 4 + m, near, r2.at[r, h, m, :, :, pl.ds(m * Q, Q)], second(h, d))

    def rs2(r, h):
        p = part.at[r]
        for m in range(2, 6):
            rmsgs[r, h, m].wait_recv()
        own = row(p, h, 0, cols(h))
        q[r, h] = (own[...].astype(F32) + r2[r, h, 0].astype(F32) + r2[r, h, 1].astype(F32)).astype(BF16)

        for m, d in ((0, 2), (1, 1), (2, -1)):
            place = at(0, d)[1] if h == 0 else at(d, 0)[0]
            rs_send_msg(r, h, 6 + m, q.at[r, h, place], r4.at[r, h, m], first(h, d))

    def rs4(r, h):
        for m in range(6, 9):
            rmsgs[r, h, m].wait_recv()
        total = q[r, h, x if h == 0 else y].astype(F32)
        for m in range(3):
            total += r4[r, h, m].astype(F32)
        return total

    rs_stages = (rs0, rs1, rs2)

    def scatter(r, stage):
        for h in range(2):
            rs_stages[stage](r, h)

    def rows(k):
        return ag[k].reshape(tokens, D)

    def prep_nb():
        c_saved.wait()
        kept = tok[0].astype(F32)
        ag[NB, y, x] = (kept * inv_rms(kept)).astype(BF16)

    def prep_ct():
        c_grads.wait()
        pl.when(has_next)(x_grads.wait_recv)
        ag[CT, y, x] = jnp.where(has_next, tok[4], tok[2])

    def prep_nf():
        c_acts.wait()
        pl.when(has_last)(x_acts.wait_recv)
        tok[1] = jnp.where(has_last, tok[3], tok[1])
        inputs = tok[1].astype(F32)
        ag[NF, y, x] = (inputs * inv_rms(inputs)).astype(BF16)

    def make_pre():
        c_win.wait()
        exchange[2].wait_recv()
        for c in range(2):
            value, grad = gelu_and_slope(nt(rows(NB), win[c]))
            hid[c] = value.astype(BF16)
            slope[c] = grad

    def make_dpre():
        c_wout.wait()
        exchange[3].wait_recv()
        for c in range(2):
            dpre[c] = (nt(rows(CT), wout[c]) * slope[c]).astype(BF16)

    def make_bwd(h):
        for s in range(2):
            csl = cols(h, s)
            part[BWD, :, :, :, csl] = (
                (nn(dpre[0], win[0, :, csl]) + nn(dpre[1], win[1, :, csl])).astype(BF16).reshape(4, 4, 16, Q)
            )
        rs0(BWD, h)

    def make_hidden():
        for c in range(2):
            fwd_hid[c] = gelu(nt(rows(NF), win[c])).astype(BF16)

    def make_fwd(h):
        for s in range(2):
            csl = cols(h, s)
            part[FWD, :, :, :, csl] = (
                (nn(fwd_hid[0], wout[0, :, csl]) + nn(fwd_hid[1], wout[1, :, csl])).astype(BF16).reshape(4, 4, 16, Q)
            )
        rs0(FWD, h)

    def give_gin():
        gin_s[...] = tn(dpre[1], rows(NB)).astype(BF16)
        exchange[4] = send(gin_s, gin_r, ex_send.at[4], ex_recv.at[4], sibling)

    def give_gout():
        gout_s[...] = tn(hid[1], rows(CT)).astype(BF16)
        exchange[5] = send(gout_s, gout_r, ex_send.at[5], ex_recv.at[5], sibling)

    def keep_grads():
        o_gin[0] = tn(dpre[0], rows(NB)).astype(BF16)
        o_gout[0] = tn(hid[0], rows(CT)).astype(BF16)

    def add_grads():
        exchange[4].wait_recv()
        o_gin[0] = (o_gin[0].astype(F32) + gin_r[...].astype(F32)).astype(BF16)
        exchange[5].wait_recv()
        o_gout[0] = (o_gout[0].astype(F32) + gout_r[...].astype(F32)).astype(BF16)

    exchange = {}

    def meet_sibling():
        exchange[2] = send(w_in.at[0], win.at[1], ex_send.at[2], ex_recv.at[2], sibling)
        exchange[3] = send(w_out.at[0], wout.at[1], ex_send.at[3], ex_recv.at[3], sibling)

    def finish_bwd():
        d_normed = jnp.concatenate([rs4(BWD, 0), rs4(BWD, 1)], axis=-1)
        kept = tok[0].astype(F32)
        scale = inv_rms(kept)
        inner = jnp.mean(d_normed * kept, axis=-1, keepdims=True)
        back = scale * d_normed - kept * (scale * scale * scale * inner)
        o_grads[0] = (ag[CT, y, x].astype(F32) + back).astype(BF16)

    def finish_fwd():
        o_acts[0] = (tok[1].astype(F32) + jnp.concatenate([rs4(FWD, 0), rs4(FWD, 1)], axis=-1)).astype(BF16)

    prep_nb()
    gather(NB, 0)
    meet_sibling()
    gather(NB, 1)
    prep_ct()
    gather(CT, 0)
    gather(NB, 2)
    prep_nf()
    gather(NF, 0)
    gather(CT, 1)
    gather(NB, 3)
    gather(NF, 1)
    gather(NB, 4)
    gather(CT, 2)
    gather(NF, 2)
    gather(CT, 3)
    gather(NB, 5)
    gather(CT, 4)
    gather(NF, 3)
    gather(NB, 6)
    gather(CT, 5)
    gather(NF, 4)
    make_pre()
    gather(CT, 6)
    gather(NF, 5)
    make_dpre()
    make_bwd(0)
    make_bwd(1)
    gather(NF, 6)
    make_hidden()
    make_fwd(0)
    make_fwd(1)
    scatter(BWD, 1)
    give_gin()
    scatter(FWD, 1)
    give_gout()
    scatter(BWD, 2)
    scatter(FWD, 2)
    keep_grads()
    add_grads()
    finish_bwd()
    finish_fwd()
    pl.when(has_next)(x_acts.wait_send)
    pl.when(has_last)(x_grads.wait_send)
    for copy in sent:
        copy.wait_send()


def store(*refs):
    copies = [pltpu.make_async_copy(refs[i], refs[4 + i], refs[8].at[i]) for i in range(4)]
    for copy in copies:
        copy.start()
    for copy in copies:
        copy.wait()


def shards(n_z, acts, grads, saved, w_in, w_out):
    _, T, D = acts.shape
    w_in = jnp.swapaxes(w_in, 1, 2)
    U = w_in.shape[1]
    H, Q = D // 2, D // 4
    vmem = pltpu.VMEM
    sem = pltpu.SemaphoreType.DMA
    anywhere = pl.BlockSpec(memory_space=pl.ANY)
    whole = pl.BlockSpec(memory_space=pltpu.VMEM)
    tokens = 16 * T
    results = pl.pallas_call(
        functools.partial(kernel, n_z),
        out_shape=(
            vmem(acts.shape, BF16),
            vmem(acts.shape, BF16),
            vmem(w_in.shape, BF16),
            vmem(w_out.shape, BF16),
        ),
        in_specs=[anywhere] * 5,
        out_specs=(whole,) * 4,
        scratch_shapes=[
            vmem((5, T, D), BF16),
            vmem((3, 4, 4, T, D), BF16),
            vmem((2, U, D), BF16),
            vmem((2, U, D), BF16),
            vmem((2, 4, 4, T, D), BF16),
            vmem((2, 2, 2, 4, T, Q), BF16),
            vmem((2, 2, 2, 4, T, H), BF16),
            vmem((2, 2, 3, T, H), BF16),
            vmem((2, 2, 4, T, H), BF16),
            vmem((2, tokens, U), BF16),
            vmem((2, tokens, U), BF16),
            vmem((2, tokens, U), BF16),
            vmem((2, tokens, U), F32),
            vmem((U, D), BF16),
            vmem((U, D), BF16),
            vmem((U, D), BF16),
            vmem((U, D), BF16),
            sem((5,)),
            sem((3, 2, 20)),
            sem((3, 2, 20)),
            sem((2, 2, 9)),
            sem((2, 2, 9)),
            sem((6,)),
            sem((6,)),
        ],
        compiler_params=pltpu.CompilerParams(
            collective_id=0, has_side_effects=True, vmem_limit_bytes=56 * 1024 * 1024
        ),
    )(acts, grads, saved, w_in, w_out)
    out_acts, out_grads, grad_in, grad_out = pl.pallas_call(
        store,
        out_shape=tuple(jax.ShapeDtypeStruct(r.shape, r.dtype) for r in results),
        in_specs=[anywhere] * 4,
        out_specs=(anywhere,) * 4,
        scratch_shapes=[sem((4,))],
        compiler_params=pltpu.CompilerParams(vmem_limit_bytes=1024 * 1024),
    )(*results)
    return out_acts, out_grads, jnp.swapaxes(grad_in, 1, 2), grad_out


def solution(mesh):
    rows_split = P("section", ("tensor", "dp"), None)
    columns_split = P("section", None, ("tensor", "dp"))
    return jax.shard_map(
        functools.partial(shards, mesh.shape["section"] // 2),
        mesh=mesh,
        in_specs=(rows_split, rows_split, rows_split, columns_split, rows_split),
        out_specs=(rows_split, rows_split, columns_split, rows_split),
        check_vma=False,
    )
```

```python
import functools

import jax
import jax.numpy as jnp
from jax import lax
from jax.experimental import pallas as pl
from jax.experimental.pallas import tpu as pltpu
from jax.sharding import PartitionSpec as P

MESH = pl.DeviceIdType.MESH
F32, BF16 = jnp.float32, jnp.bfloat16
EPS = 1e-05
NB, CT, NF = 0, 1, 2
BWD, FWD = 0, 1
GELU_A, GELU_B = 0.7978845608028654, 0.044715


def inv_rms(values):
    return lax.rsqrt(jnp.mean(values * values, axis=-1, keepdims=True) + EPS)


def gelu(v):
    return 0.5 * v * (1.0 + jnp.tanh(GELU_A * (v + GELU_B * (v * v * v))))


def gelu_and_slope(v):
    square = v * v
    t = jnp.tanh(GELU_A * (v + GELU_B * (v * square)))
    value = 0.5 * v * (1.0 + t)
    slope = 0.5 * (1.0 + t) + 0.5 * v * (1.0 - t * t) * (GELU_A * (1.0 + 3.0 * GELU_B * square))
    return value, slope


def nn(a, b):
    return jnp.dot(a, b, preferred_element_type=F32)


def nt(a, b):
    return lax.dot_general(a, b, (((1,), (1,)), ((), ())), preferred_element_type=F32)


def tn(a, b):
    return lax.dot_general(a, b, (((0,), (0,)), ((), ())), preferred_element_type=F32)


def kernel(
    n_z, acts, grads, saved, w_in, w_out, o_acts, o_grads, o_gin, o_gout,
    tok, ag, win, wout, part, r1, r2, r4, q, hid, fwd_hid, dpre, slope, gin_s, gin_r, gout_s, gout_r,
    loc_sem, ag_send, ag_recv, rs_send, rs_recv, ex_send, ex_recv,
):
    sec, y, dp = lax.axis_index("section"), lax.axis_index("tensor"), lax.axis_index("dp")
    z = lax.rem(sec, n_z)
    x_hi = sec // n_z
    x = 2 * x_hi + dp // 2
    core = lax.rem(dp, 2)
    D = ag.shape[-1]
    H, Q = D // 2, D // 4
    tokens = 16 * ag.shape[3]

    def at(dy, dx):
        return lax.rem(y + dy + 4, 4), lax.rem(x + dx + 4, 4)

    def chip(dy, dx):
        yy, xx = at(dy, dx)
        return ((xx // 2) * n_z + z, yy, 2 * lax.rem(xx, 2) + core)

    def plane(dz):
        return (sec + dz, y, dp)

    sibling = (sec, y, dp + 1 - 2 * core)

    sent = []

    def send(src, dst, ssem, rsem, dev):
        copy = pltpu.make_async_remote_copy(
            src_ref=src, dst_ref=dst, send_sem=ssem, recv_sem=rsem, device_id=dev, device_id_type=MESH
        )
        copy.start()
        sent.append(copy)
        return copy

    has_next, has_last = z < n_z - 1, z > 0
    barrier = pltpu.get_barrier_semaphore()

    def greet(dev):
        pl.semaphore_signal(barrier, inc=1, device_id=dev, device_id_type=MESH)

    pl.when(has_next)(lambda: greet(plane(1)))
    pl.when(has_last)(lambda: greet(plane(-1)))
    for dev in (chip(0, 1), chip(0, -1), chip(1, 0), chip(-1, 0), sibling):
        greet(dev)

    def local(src, dst, i):
        copy = pltpu.make_async_copy(src, dst, loc_sem.at[i])
        copy.start()
        return copy

    c_saved = local(saved.at[0], tok.at[0], 0)
    c_acts = local(acts.at[0], tok.at[1], 1)
    c_grads = local(grads.at[0], tok.at[2], 2)
    c_win = local(w_in.at[0], win.at[0], 3)
    c_wout = local(w_out.at[0], wout.at[0], 4)

    c_saved.wait()
    kept = tok[0].astype(F32)
    ag[NB, y, x] = (kept * inv_rms(kept)).astype(BF16)

    pl.semaphore_wait(barrier, 5 + jnp.where(has_next, 1, 0) + jnp.where(has_last, 1, 0))

    def shifted(src, dst, n, dev):
        return pltpu.make_async_remote_copy(
            src_ref=src, dst_ref=dst, send_sem=ex_send.at[n], recv_sem=ex_recv.at[n], device_id=dev,
            device_id_type=MESH,
        )

    x_acts = shifted(acts.at[0], tok.at[3], 0, plane(1))
    x_grads = shifted(grads.at[0], tok.at[4], 1, plane(-1))
    pl.when(has_next)(x_acts.start)
    pl.when(has_last)(x_grads.start)

    def cols(h, part_no=None):
        if part_no is None:
            return pl.ds(h * H, H)
        return pl.ds(h * H + part_no * Q, Q)

    def first(h, d):
        return (0, d) if h == 0 else (d, 0)

    def second(h, d):
        return (d, 0) if h == 0 else (0, d)

    def slot(h, df, ds):
        return at(ds, df) if h == 0 else at(df, ds)

    msgs = {}

    def ag_send_msg(k, h, m, df, ds, sub, dev):
        yy, xx = slot(h, df, ds)
        ref = ag.at[k, yy, xx, :, cols(h, sub)]
        msgs[k, h, m] = send(ref, ref, ag_send.at[k, h, m], ag_recv.at[k, h, m], chip(*dev))

    J = (0, -1, 1, 2)

    def ag0(k, h):
        ag_send_msg(k, h, 0, 0, 0, None, first(h, 1))
        ag_send_msg(k, h, 1, 0, 0, None, first(h, -1))
        ag_send_msg(k, h, 4, 0, 0, None, second(h, 1))
        ag_send_msg(k, h, 5, 0, 0, None, second(h, -1))

    def ag1(k, h):
        for m, d in ((0, -1), (1, 1)):
            msgs[k, h, m].wait_recv()
            ag_send_msg(k, h, 2 + m, d, 0, m, first(h, -d))
            j = J.index(d)
            ag_send_msg(k, h, 4 + 2 * j, d, 0, None, second(h, 1))
            ag_send_msg(k, h, 5 + 2 * j, d, 0, None, second(h, -1))

    def ag_forward(k, h, j):
        for m, d in ((0, -1), (1, 1)):
            msgs[k, h, 4 + 2 * j + m].wait_recv()
            ag_send_msg(k, h, 12 + 2 * j + m, J[j], d, m, second(h, -d))

    def ag2(k, h):
        ag_forward(k, h, 0)

    def ag3(k, h):
        msgs[k, h, 2].wait_recv()
        msgs[k, h, 3].wait_recv()
        ag_send_msg(k, h, 10, 2, 0, None, second(h, 1))
        ag_send_msg(k, h, 11, 2, 0, None, second(h, -1))

    def ag4(k, h):
        ag_forward(k, h, 1)
        ag_forward(k, h, 2)

    def ag5(k, h):
        ag_forward(k, h, 3)

    def ag6(k, h):
        for m in range(12, 20):
            msgs[k, h, m].wait_recv()


    def row(ref, h, d, csl):
        if h == 0:
            return ref.at[at(d, 0)[0], :, :, csl]
        return ref.at[:, at(0, d)[1], :, csl]

    rmsgs = {}

    def rs_send_msg(r, h, m, src, dst, dev):
        rmsgs[r, h, m] = send(src, dst, rs_send.at[r, h, m], rs_recv.at[r, h, m], chip(*dev))

    def rs0(r, h):
        p = part.at[r]
        for m, d in ((0, 1), (1, -1)):
            rs_send_msg(r, h, m, row(p, h, 2, cols(h, m)), r1.at[r, h, m], second(h, d))
        for m, d in ((0, 1), (1, -1)):
            rs_send_msg(
                r, h, 2 + m, row(p, h, d, cols(h, 1 - m)), r2.at[r, h, m, :, :, pl.ds((1 - m) * Q, Q)], second(h, d)
            )

    def rs1(r, h):
        p = part.at[r]
        for m, d in ((0, 1), (1, -1)):
            rmsgs[r, h, m].wait_recv()
            near = row(p, h, d, cols(h, m))
            near[...] = (near[...].astype(F32) + r1[r, h, m].astype(F32)).astype(BF16)
            rs_send_msg(r, h, 4 + m, near, r2.at[r, h, m, :, :, pl.ds(m * Q, Q)], second(h, d))

    def rs2(r, h):
        p = part.at[r]
        for m in range(2, 6):
            rmsgs[r, h, m].wait_recv()
        own = row(p, h, 0, cols(h))
        q[r, h] = (own[...].astype(F32) + r2[r, h, 0].astype(F32) + r2[r, h, 1].astype(F32)).astype(BF16)

        for m, d in ((0, 2), (1, 1), (2, -1)):
            place = at(0, d)[1] if h == 0 else at(d, 0)[0]
            rs_send_msg(r, h, 6 + m, q.at[r, h, place], r4.at[r, h, m], first(h, d))

    def rs4(r, h):
        for m in range(6, 9):
            rmsgs[r, h, m].wait_recv()
        total = q[r, h, x if h == 0 else y].astype(F32)
        for m in range(3):
            total += r4[r, h, m].astype(F32)
        return total


    def rows(k):
        return ag[k].reshape(tokens, D)

    def prep_ct():
        c_grads.wait()
        pl.when(has_next)(x_grads.wait_recv)
        ag[CT, y, x] = jnp.where(has_next, tok[4], tok[2])

    def prep_nf():
        c_acts.wait()
        pl.when(has_last)(x_acts.wait_recv)
        tok[1] = jnp.where(has_last, tok[3], tok[1])
        inputs = tok[1].astype(F32)
        ag[NF, y, x] = (inputs * inv_rms(inputs)).astype(BF16)

    def make_pre():
        c_win.wait()
        exchange[2].wait_recv()
        for c in range(2):
            value, grad = gelu_and_slope(nt(rows(NB), win[c]))
            hid[c] = value.astype(BF16)
            slope[c] = grad

    def make_dpre():
        c_wout.wait()
        exchange[3].wait_recv()
        for c in range(2):
            dpre[c] = (nt(rows(CT), wout[c]) * slope[c]).astype(BF16)

    def make_bwd(h):
        for s in range(2):
            csl = cols(h, s)
            part[BWD, :, :, :, csl] = (
                (nn(dpre[0], win[0, :, csl]) + nn(dpre[1], win[1, :, csl])).astype(BF16).reshape(4, 4, 16, Q)
            )
        rs0(BWD, h)

    def make_hidden():
        for c in range(2):
            fwd_hid[c] = gelu(nt(rows(NF), win[c])).astype(BF16)

    def make_fwd(h):
        for s in range(2):
            csl = cols(h, s)
            part[FWD, :, :, :, csl] = (
                (nn(fwd_hid[0], wout[0, :, csl]) + nn(fwd_hid[1], wout[1, :, csl])).astype(BF16).reshape(4, 4, 16, Q)
            )
        rs0(FWD, h)

    def give_gin():
        gin_s[...] = tn(dpre[1], rows(NB)).astype(BF16)
        exchange[4] = send(gin_s, gin_r, ex_send.at[4], ex_recv.at[4], sibling)

    def give_gout():
        gout_s[...] = tn(hid[1], rows(CT)).astype(BF16)
        exchange[5] = send(gout_s, gout_r, ex_send.at[5], ex_recv.at[5], sibling)

    def keep_grads():
        o_gin[0] = tn(dpre[0], rows(NB)).astype(BF16)
        o_gout[0] = tn(hid[0], rows(CT)).astype(BF16)

    def add_grads():
        exchange[4].wait_recv()
        o_gin[0] = (o_gin[0].astype(F32) + gin_r[...].astype(F32)).astype(BF16)
        exchange[5].wait_recv()
        o_gout[0] = (o_gout[0].astype(F32) + gout_r[...].astype(F32)).astype(BF16)

    exchange = {}

    def meet_sibling():
        exchange[2] = send(w_in.at[0], win.at[1], ex_send.at[2], ex_recv.at[2], sibling)
        exchange[3] = send(w_out.at[0], wout.at[1], ex_send.at[3], ex_recv.at[3], sibling)

    def finish_bwd():
        d_normed = jnp.concatenate([rs4(BWD, 0), rs4(BWD, 1)], axis=-1)
        kept = tok[0].astype(F32)
        scale = inv_rms(kept)
        inner = jnp.mean(d_normed * kept, axis=-1, keepdims=True)
        back = scale * d_normed - kept * (scale * scale * scale * inner)
        o_grads[0] = (ag[CT, y, x].astype(F32) + back).astype(BF16)

    def finish_fwd():
        o_acts[0] = (tok[1].astype(F32) + jnp.concatenate([rs4(FWD, 0), rs4(FWD, 1)], axis=-1)).astype(BF16)

    ag0(NB, 0)
    ag0(NB, 1)
    meet_sibling()
    ag1(NB, 0)
    ag1(NB, 1)
    prep_ct()
    ag0(CT, 0)
    ag0(CT, 1)
    ag2(NB, 0)
    ag2(NB, 1)
    prep_nf()
    ag0(NF, 0)
    ag0(NF, 1)
    ag1(CT, 0)
    ag1(CT, 1)
    ag3(NB, 0)
    ag3(NB, 1)
    ag1(NF, 0)
    ag1(NF, 1)
    ag4(NB, 0)
    ag4(NB, 1)
    ag2(CT, 0)
    ag2(CT, 1)
    ag2(NF, 0)
    ag2(NF, 1)
    ag3(CT, 0)
    ag3(CT, 1)
    ag5(NB, 0)
    ag5(NB, 1)
    ag4(CT, 0)
    ag4(CT, 1)
    ag3(NF, 0)
    ag3(NF, 1)
    ag6(NB, 0)
    ag6(NB, 1)
    ag5(CT, 0)
    ag5(CT, 1)
    ag4(NF, 0)
    ag4(NF, 1)
    make_pre()
    ag6(CT, 0)
    ag6(CT, 1)
    ag5(NF, 0)
    ag5(NF, 1)
    make_dpre()
    make_bwd(0)
    make_bwd(1)
    give_gin()
    ag6(NF, 0)
    ag6(NF, 1)
    make_hidden()
    make_fwd(0)
    make_fwd(1)
    rs1(BWD, 0)
    rs1(BWD, 1)
    give_gout()
    rs1(FWD, 0)
    rs1(FWD, 1)
    keep_grads()
    rs2(BWD, 0)
    rs2(BWD, 1)
    rs2(FWD, 0)
    rs2(FWD, 1)
    add_grads()
    finish_bwd()
    finish_fwd()
    pl.when(has_next)(x_acts.wait_send)
    pl.when(has_last)(x_grads.wait_send)
    for copy in sent:
        copy.wait_send()


def store(*refs):
    copies = []
    for n, piece in enumerate((refs[0].shape[1], refs[1].shape[1], 48, 48)):
        for at in range(0, refs[n].shape[1], piece):
            rows = pl.ds(at, piece)
            copies.append((refs[n].at[:, rows], refs[4 + n].at[:, rows]))
    copies = [pltpu.make_async_copy(src, dst, refs[8].at[n]) for n, (src, dst) in enumerate(copies)]
    for copy in copies:
        copy.start()
    for copy in copies:
        copy.wait()


def shards(n_z, acts, grads, saved, w_in, w_out):
    _, T, D = acts.shape
    w_in = jnp.swapaxes(w_in, 1, 2)
    U = w_in.shape[1]
    H, Q = D // 2, D // 4
    vmem = pltpu.VMEM
    sem = pltpu.SemaphoreType.DMA
    anywhere = pl.BlockSpec(memory_space=pl.ANY)
    whole = pl.BlockSpec(memory_space=pltpu.VMEM)
    tokens = 16 * T
    results = pl.pallas_call(
        functools.partial(kernel, n_z),
        out_shape=(
            vmem(acts.shape, BF16),
            vmem(acts.shape, BF16),
            vmem(w_in.shape, BF16),
            vmem(w_out.shape, BF16),
        ),
        in_specs=[anywhere] * 5,
        out_specs=(whole,) * 4,
        scratch_shapes=[
            vmem((5, T, D), BF16),
            vmem((3, 4, 4, T, D), BF16),
            vmem((2, U, D), BF16),
            vmem((2, U, D), BF16),
            vmem((2, 4, 4, T, D), BF16),
            vmem((2, 2, 2, 4, T, Q), BF16),
            vmem((2, 2, 2, 4, T, H), BF16),
            vmem((2, 2, 3, T, H), BF16),
            vmem((2, 2, 4, T, H), BF16),
            vmem((2, tokens, U), BF16),
            vmem((2, tokens, U), BF16),
            vmem((2, tokens, U), BF16),
            vmem((2, tokens, U), F32),
            vmem((U, D), BF16),
            vmem((U, D), BF16),
            vmem((U, D), BF16),
            vmem((U, D), BF16),
            sem((5,)),
            sem((3, 2, 20)),
            sem((3, 2, 20)),
            sem((2, 2, 9)),
            sem((2, 2, 9)),
            sem((6,)),
            sem((6,)),
        ],
        compiler_params=pltpu.CompilerParams(
            collective_id=0, has_side_effects=True, vmem_limit_bytes=56 * 1024 * 1024
        ),
    )(acts, grads, saved, w_in, w_out)
    out_acts, out_grads, grad_in, grad_out = pl.pallas_call(
        store,
        out_shape=tuple(jax.ShapeDtypeStruct(r.shape, r.dtype) for r in results),
        in_specs=[anywhere] * 4,
        out_specs=(anywhere,) * 4,
        scratch_shapes=[sem((2 + 2 * (U // 48),))],
        compiler_params=pltpu.CompilerParams(vmem_limit_bytes=1024 * 1024),
    )(*results)
    return out_acts, out_grads, jnp.swapaxes(grad_in, 1, 2), grad_out


def solution(mesh):
    rows_split = P("section", ("tensor", "dp"), None)
    columns_split = P("section", None, ("tensor", "dp"))
    return jax.shard_map(
        functools.partial(shards, mesh.shape["section"] // 2),
        mesh=mesh,
        in_specs=(rows_split, rows_split, rows_split, columns_split, rows_split),
        out_specs=(rows_split, rows_split, columns_split, rows_split),
        check_vma=False,
    )
```
